128 devices in a mesh: gx: 8 (over x, core), gy: 16 (over z, y).
Axes of the slice: x: 4, y: 4, z: 4, core: 2. Of those that a mesh axis runs over, the one named last changes fastest.
Arguments:
- leaf_density: bfloat16 [65536, 128], P(('gx', 'gy')), may hold values from -6 to 6
- mid_density: bfloat16 [8192, 128], P(('gx', 'gy')), may hold values from -6 to 6
- top_density: bfloat16 [1024, 128], P(('gx', 'gy')), may hold values from -6 to 6
- leaf_lists: int32 [65536, 316], P(('gx', 'gy')), may hold values from -1 to 1535, as said below
- mid_lists: int32 [8192, 316], P(('gx', 'gy')), may hold values from -1 to 191, as said below
- top_lists: int32 [1024, 316], P(('gx', 'gy')), may hold values from -1 to 23, as said below
- operators: bfloat16 [316, 128, 128], replicated, may hold values from -0.0390625 to 0.0390625
- positions: float32 [32768, 3, 256], P(('gx', 'gy')), may hold values from 0 to 1
- charges: float32 [32768, 256], P(('gx', 'gy')), may hold values from -0.24 to 0.24
- pairs: int32 [65536, 2], P(('gx', 'gy')), may hold values from 0 to 32767, as said below
Outputs:
- leaf_local: float32 [65536, 128], P(('gx', 'gy'))
- mid_local: float32 [8192, 128], P(('gx', 'gy'))
- top_local: float32 [1024, 128], P(('gx', 'gy'))
- near_potential: float32 [32768, 256], P(('gx', 'gy'))
The draws below stay inside these ranges and needn't reach their ends.
Inputs may be any that keep to these rules, and one draw needn't show every extreme that they name: `leaf_lists`: boxes of a level are owned 512, 64 or 8 a device in order, devices ordered by gx then gy; every entry e >= 0 names a box of the same level owned by the listing box's owner or a device next to it in that order, and that box exists; -1 marks an empty slot. `mid_lists`: as for leaf_lists, at this level. `top_lists`: as for leaf_lists, at this level. `pairs`: blocks are owned 256 a device in order; both blocks of a pair in the rows of one device are owned by that device or a device next to it in the order of gx then gy.
All inputs are finite; a program needn't handle non-finite values.
Results may differ from the reference program's by a relative error of at most 0.0003.
Values may be sent and summed in bfloat16 or wider, within the bound.
No kernel may reach another device: no remote copies, remote signals or barrier semaphores. Data moves between devices by JAX's collectives and lax.ppermute only.
A program may use at most 256 MiB of HBM per device.

```python
import jax
import jax.numpy as jnp
from jax import lax

EQUIV_PTS = 128
VECTORS = 316
LEAF_DEV = 512
BLK_DEV = 256
BLOCK_PTS = 256
PAIRS_DEV = 512
LEAF_BOXES = 65536
MID_BOXES = 8192
TOP_BOXES = 1024
BLOCKS = 32768
PAIRS = 65536


def neighbour_list(key, count, per_dev):
    owner = jnp.arange(count, dtype=jnp.int32) // per_dev
    owner = jnp.broadcast_to(owner[:, None], (count, VECTORS))
    key_a, key_b = jax.random.split(key)
    present = jax.random.randint(key_a, (count, VECTORS), 0, 5) < 3
    picked = (owner - 1) * per_dev + jax.random.randint(key_b, (count, VECTORS), 0, 3 * per_dev)
    picked = jnp.clip(picked, 0, count - 1)
    relative = picked - (owner - 1) * per_dev
    return jnp.where(present, relative, -1).astype(jnp.int32)


def draw_leaf_lists(key, part):
    key = jax.random.fold_in(key, 11)
    return neighbour_list(key, LEAF_BOXES, LEAF_DEV)


def draw_mid_lists(key, part):
    key = jax.random.fold_in(key, 12)
    return neighbour_list(key, MID_BOXES, LEAF_DEV // 8)


def draw_top_lists(key, part):
    key = jax.random.fold_in(key, 13)
    return neighbour_list(key, TOP_BOXES, LEAF_DEV // 64)


def draw_pairs(key, part):
    key = jax.random.fold_in(key, 14)
    worker = jnp.arange(PAIRS, dtype=jnp.int32) // PAIRS_DEV
    worker = jnp.broadcast_to(worker[:, None], (PAIRS, 2))
    picked = (worker - 1) * BLK_DEV + jax.random.randint(key, (PAIRS, 2), 0, 3 * BLK_DEV)
    return jnp.clip(picked, 0, BLOCKS - 1).astype(jnp.int32)


def block_levels(own_key, shape, pieces, least, high):
    def one(position, parts):
        heights = jax.random.uniform(jax.random.fold_in(jax.random.fold_in(own_key, 6), position), (parts,), jnp.float32, least / len(pieces), high / len(pieces))
        return jnp.repeat(jnp.exp(heights), shape[position] // parts).reshape((-1,) + (1,) * (len(shape) - position - 1))

    factor_of = one(*pieces[0])
    for cut in pieces[1:]:
        factor_of = factor_of * one(*cut)
    return factor_of


def centred(key, extent, spread, reach, cuts=(), kind=jnp.bfloat16):
    entries = spread * jax.random.normal(key, extent, jnp.float32)
    if cuts:
        entries = entries * block_levels(key, extent, cuts, -0.22, 0.18)
    return jnp.clip(entries, -reach, reach).astype(kind)


def setup_inputs(seed: int = 0) -> dict:
    key_list = jax.random.split(jax.random.key(seed), 11)
    leaf_density = centred(key_list[0], (LEAF_BOXES, EQUIV_PTS), 1.0, 6.0, ((0, 128),))
    mid_density = centred(key_list[1], (MID_BOXES, EQUIV_PTS), 1.0, 6.0, ((0, 128),))
    top_density = centred(key_list[2], (TOP_BOXES, EQUIV_PTS), 1.0, 6.0, ((0, 128),))
    leaf_lists = draw_leaf_lists(jax.random.fold_in(key_list[10], 71), 0)
    mid_lists = draw_mid_lists(jax.random.fold_in(key_list[10], 71), 0)
    top_lists = draw_top_lists(jax.random.fold_in(key_list[10], 71), 0)
    operators = centred(key_list[6], (VECTORS, EQUIV_PTS, EQUIV_PTS), (EQUIV_PTS * VECTORS // 2) ** -0.5, 0.0390625)
    positions = jnp.clip(1.0 * jax.random.uniform(key_list[7], (BLOCKS, 3, BLOCK_PTS), jnp.float32) ** block_levels(key_list[7], (BLOCKS, 3, BLOCK_PTS), ((0, 128),), -0.2, 0.2), 0.0, 1.0)
    charges = centred(key_list[8], (BLOCKS, BLOCK_PTS), 0.03, 0.24, ((0, 128),), jnp.float32)
    pairs = draw_pairs(jax.random.fold_in(key_list[10], 71), 0)
    return {"leaf_density": leaf_density, "mid_density": mid_density, "top_density": top_density, "leaf_lists": leaf_lists, "mid_lists": mid_lists, "top_lists": top_lists, "operators": operators, "positions": positions, "charges": charges, "pairs": pairs}


soften_sq = 0.0025

def translate(density, lists, operators, per_dev):
    count = density.shape[0]
    width = min(count, 256)
    flat = operators.reshape(VECTORS * EQUIV_PTS, EQUIV_PTS)
    owner = jnp.arange(count, dtype=jnp.int32) // per_dev
    base = ((owner - 1) * per_dev).astype(jnp.int32)

    def one_block(item):
        rows, start = item
        valid = rows >= 0
        target = jnp.where(valid, rows + start[:, None], 0).astype(jnp.int32)
        picked = density[target] * valid[..., None].astype(density.dtype)
        return jnp.dot(picked.reshape(rows.shape[0], VECTORS * EQUIV_PTS), flat, preferred_element_type=jnp.float32)
    result = lax.map(one_block, (lists.reshape(count // width, width, VECTORS), base.reshape(count // width, width)))
    return result.reshape(count, EQUIV_PTS)

def reference(leaf_density, mid_density, top_density, leaf_lists, mid_lists, top_lists, operators, positions, charges, pairs):
    leaf_local = translate(leaf_density, leaf_lists, operators, LEAF_DEV)
    mid_local = translate(mid_density, mid_lists, operators, LEAF_DEV // 8)
    top_local = translate(top_density, top_lists, operators, LEAF_DEV // 64)
    packed = jnp.concatenate([positions, charges[:, None, :]], axis=1)
    group = 64

    def one_group(batch):
        target = packed[batch[:, 0]]
        source = packed[batch[:, 1]]
        diff = target[:, :3, :, None] - source[:, :3, None, :]
        dist_sq = lax.optimization_barrier(jnp.sum(diff * diff, axis=1))
        kernel = lax.rsqrt(dist_sq + soften_sq)
        return lax.optimization_barrier(jnp.sum(kernel * source[:, 3, None, :], axis=2))
    terms = lax.map(one_group, pairs.reshape(PAIRS // group, group, 2)).reshape(PAIRS, BLOCK_PTS)
    near_potential = jnp.zeros((BLOCKS, BLOCK_PTS), jnp.float32).at[pairs[:, 0]].add(terms)
    return (leaf_local, mid_local, top_local, near_potential)
```

```python
import functools

import jax
import jax.numpy as jnp
from jax import lax
from jax.experimental import pallas as pl
from jax.experimental.pallas import tpu as pltpu
from jax.sharding import PartitionSpec as P

soften_sq = 0.0025
AXES = ("gx", "gy")
F8 = jnp.float8_e4m3fn
BF16 = jnp.bfloat16
F32 = jnp.float32
GROUP = 4
PAIR_UNROLL = 8


def halo(block):
    count = lax.axis_size(AXES)
    before = lax.ppermute(block, AXES, [(i, i + 1) for i in range(count - 1)])
    after = lax.ppermute(block, AXES, [(i + 1, i) for i in range(count - 1)])
    return before, after


def power_scale(largest):
    scale, inverse = jnp.float32(2.0**-119), jnp.float32(2.0**119)
    for bits in (64, 64, 32, 16, 8, 4, 2, 1):
        fits = largest * (scale * 2.0**bits) <= 448.0
        scale = jnp.where(fits, scale * 2.0**bits, scale)
        inverse = jnp.where(fits, inverse * 2.0**-bits, inverse)
    return scale, inverse


def split_table(rows, scale):
    scaled = rows * scale
    high = scaled.astype(F8)
    low = ((scaled - high.astype(F32)) * 16.0).astype(F8)
    return jnp.concatenate([high, low], axis=1)


def translate_kernel(
    sizes, lists_ref, prev_ref, own_ref, next_ref, op_ref, leaf_ref, mid_ref, top_ref,
    table, small_table, total, inverses,
):
    leaf, mid, top = sizes
    points = own_ref.shape[1]
    small = total.shape[0] - leaf
    step = pl.program_id(0)

    @pl.when(step == 0)
    def _():
        total[...] = jnp.zeros_like(total)
        parts = [ref[...].astype(F32) for ref in (prev_ref, own_ref, next_ref)]
        level, at = [], 0
        for i, size in enumerate(sizes):
            rows = jnp.concatenate([p[at : at + size] for p in parts], axis=0)
            scale, inverse = power_scale(jnp.max(jnp.abs(rows)))
            inverses[i] = inverse
            level.append((rows, scale))
            at += size
        table[...] = split_table(*level[0])
        pad = small_table.shape[0] - 3 * (mid + top)
        small_rows = [split_table(*level[1]), split_table(*level[2]), jnp.zeros((pad, 2 * points), F8)]
        small_table[...] = jnp.concatenate([r.astype(F32) for r in small_rows], axis=0).astype(F8)

    lanes = lax.broadcasted_iota(jnp.int32, (1, 128), 1).astype(BF16)
    low_ids, high_ids = lanes, lanes + BF16(128)
    one, zero = BF16(1), BF16(0)
    first = step * GROUP
    chunk = lists_ref[:, pl.ds(pl.multiple_of(first // 128 * 128, 128), 128)]
    result = None
    for pair in range(GROUP // 2):
        picked = []
        for j in (2 * pair, 2 * pair + 1):
            lane = lax.rem(first + j, 128)
            column = jnp.take_along_axis(chunk, jnp.full(chunk.shape, lane, jnp.int32), axis=1)
            tile = (column >> 8).astype(BF16)
            within = (column & 255).astype(BF16)
            halves = [jnp.where(within == ids, one, zero) for ids in (low_ids, high_ids)]
            pieces = [
                jnp.where(tile[:leaf] == BF16(k), half[:leaf], zero).astype(F8)
                for k in range(table.shape[0] // 256)
                for half in halves
            ]
            parts = jnp.dot(jnp.concatenate(pieces, axis=1), table[...], preferred_element_type=F32)
            few = jnp.dot(
                jnp.concatenate([half[leaf:].astype(F8) for half in halves], axis=1),
                small_table[...],
                preferred_element_type=F32,
            )
            both = [p[:, :points] + p[:, points:] * (1.0 / 16.0) for p in (parts, few)]
            picked.append(jnp.concatenate([b.astype(BF16) for b in both], axis=0))
        weights = op_ref[2 * pair : 2 * pair + 2].reshape(2 * points, points)
        product = jnp.dot(jnp.concatenate(picked, axis=1), weights, preferred_element_type=F32)
        result = product if result is None else result + product
    total[...] += result

    @pl.when(step == pl.num_programs(0) - 1)
    def _():
        leaf_ref[...] = total[:leaf] * inverses[0]
        mid_ref[...] = total[leaf : leaf + mid] * inverses[1]
        top_ref[...] = total[leaf + mid : leaf + mid + top] * inverses[2]


def translate(densities, before, after, lists, operators):
    vectors, points, _ = operators.shape
    sizes = tuple(x.shape[0] for x in lists)
    leaf, mid, top = sizes
    small = -(-(mid + top) // 32) * 32
    width = -(-vectors // 128) * 128
    shifted = jnp.where(lists[2] >= 0, lists[2] + 3 * mid, -1)
    rows = jnp.concatenate([lists[0], lists[1], shifted], axis=0)
    rows = jnp.pad(rows, ((0, leaf + small - rows.shape[0]), (0, width - vectors)), constant_values=-1)
    boxes = sum(sizes)
    whole = lambda *shape: pl.BlockSpec(shape, lambda g: (0,) * len(shape))
    return pl.pallas_call(
        functools.partial(translate_kernel, sizes),
        grid=(vectors // GROUP,),
        in_specs=[whole(*rows.shape)]
        + [whole(boxes, points)] * 3
        + [pl.BlockSpec((GROUP, points, points), lambda g: (g, 0, 0))],
        out_specs=[whole(s, points) for s in sizes],
        out_shape=[jax.ShapeDtypeStruct((s, points), F32) for s in sizes],
        scratch_shapes=[
            pltpu.VMEM((3 * leaf, 2 * points), F8),
            pltpu.VMEM((256, 2 * points), F8),
            pltpu.VMEM((leaf + small, points), F32),
            pltpu.SMEM((3,), F32),
        ],
        compiler_params=pltpu.CompilerParams(vmem_limit_bytes=48 << 20),
        name="translate",
    )(rows, before, densities, after, operators)


def three_parts(x):
    first = x.astype(BF16).astype(F32)
    rest = x - first
    second = rest.astype(BF16).astype(F32)
    return first, second, rest - second


def near_kernel(pairs_ref, prev_ref, own_ref, next_ref, sums_ref, sources, targets):
    blocks, _, points = own_ref.shape
    row = lax.broadcasted_iota(jnp.int32, (8, points), 0)
    empty = jnp.zeros((4, points), F32)
    for place, ref in enumerate((prev_ref, own_ref, next_ref)):

        @pl.loop(0, blocks // 4)
        def _(i):
            for u in range(4):
                b = i * 4 + u
                x = ref[b]
                norm = x[0:1] * x[0:1] + x[1:2] * x[1:2] + x[2:3] * x[2:3]
                x = jnp.concatenate([x, empty], axis=0)
                sources[place * blocks + b] = jnp.where(
                    row < 4, x, jnp.where(row == 4, norm, jnp.where(row == 5, 1.0, 0.0))
                )
                targets[place * blocks + b] = jnp.where(
                    row < 3, -2.0 * x, jnp.where(row == 4, 1.0, jnp.where(row == 5, norm + soften_sq, 0.0))
                )

    sums_ref[...] = jnp.zeros_like(sums_ref)

    @pl.loop(0, pairs_ref.shape[1] // PAIR_UNROLL)
    def _(i):
        for u in range(PAIR_UNROLL):
            k = i * PAIR_UNROLL + u
            t, s = pairs_ref[0, k], pairs_ref[1, k]
            source = sources[s]
            s1, s2, s3 = three_parts(source)
            t1, t2, t3 = three_parts(targets[t])
            left = jnp.concatenate([s1, s1, s2, s2, s1, s3], axis=0).astype(BF16)
            right = jnp.concatenate([t1, t2, t1, t2, t3, t1], axis=0).astype(BF16)
            dist_sq = lax.dot_general(left, right, (((0,), (0,)), ((), ())), preferred_element_type=F32)
            inverse = lax.rsqrt(dist_sq)
            charge = jnp.broadcast_to(source[3:4], (128, points)).T
            terms = jnp.concatenate(
                [inverse[:, at : at + 128] * charge for at in range(0, points, 128)], axis=1
            )
            term = jnp.sum(jnp.sum(terms.reshape(points // 8, 8, points), axis=0), axis=0, keepdims=True)
            sums_ref[pl.ds(t, 1), :] += term


def near_sums(pairs, before, own, after):
    blocks, _, points = own.shape
    vmem = pl.BlockSpec(memory_space=pltpu.VMEM)
    return pl.pallas_call(
        near_kernel,
        in_specs=[pl.BlockSpec(memory_space=pltpu.SMEM), vmem, vmem, vmem],
        out_specs=vmem,
        out_shape=jax.ShapeDtypeStruct((3 * blocks, points), F32),
        scratch_shapes=[pltpu.VMEM((3 * blocks, 8, points), F32)] * 2,
        compiler_params=pltpu.CompilerParams(vmem_limit_bytes=48 << 20),
        name="near_sums",
    )(pairs, before, own, after)


def body(
    leaf_density,
    mid_density,
    top_density,
    leaf_lists,
    mid_lists,
    top_lists,
    operators,
    positions,
    charges,
    pairs,
):
    blocks = positions.shape[0]
    densities = jnp.concatenate([leaf_density, mid_density, top_density], axis=0)
    packed = jnp.concatenate([positions, charges[:, None, :]], axis=1)
    dens_before, dens_after = halo(densities)
    pack_before, pack_after = halo(packed)
    leaf_local, mid_local, top_local = translate(
        densities, dens_before, dens_after, (leaf_lists, mid_lists, top_lists), operators
    )
    offset = (lax.axis_index(AXES) - 1) * blocks
    sums = near_sums((pairs - offset).T, pack_before, packed, pack_after)
    count = lax.axis_size(AXES)
    from_next = lax.ppermute(sums[:blocks], AXES, [(i + 1, i) for i in range(count - 1)])
    from_prev = lax.ppermute(sums[2 * blocks :], AXES, [(i, i + 1) for i in range(count - 1)])
    near_potential = sums[blocks : 2 * blocks] + from_next + from_prev
    return (leaf_local, mid_local, top_local, near_potential)


def solution(mesh):
    rows, blocks = P(AXES, None), P(AXES, None, None)
    return jax.shard_map(
        body,
        mesh=mesh,
        in_specs=(rows, rows, rows, rows, rows, rows, P(), blocks, rows, rows),
        out_specs=(rows, rows, rows, rows),
        check_vma=False,
    )
```

```python
import functools

import jax
import jax.numpy as jnp
from jax import lax
from jax.experimental import pallas as pl
from jax.experimental.pallas import tpu as pltpu
from jax.sharding import PartitionSpec as P

soften_sq = 0.0025
AXES = ("gx", "gy")
F8 = jnp.float8_e4m3fn
BF16 = jnp.bfloat16
F32 = jnp.float32
PAIR_UNROLL = 16
SPANS = ((24, 8, 4), (1, 4, 0))
LAST_SPANS = ((3, 8, 0),)


def halo(block):
    count = lax.axis_size(AXES)
    before = lax.ppermute(block, AXES, [(i, i + 1) for i in range(count - 1)])
    after = lax.ppermute(block, AXES, [(i + 1, i) for i in range(count - 1)])
    return before, after


def power_scale(largest):
    scale, inverse = jnp.float32(2.0**-119), jnp.float32(2.0**119)
    for bits in (64, 64, 32, 16, 8, 4, 2, 1):
        fits = largest * (scale * 2.0**bits) <= 448.0
        scale = jnp.where(fits, scale * 2.0**bits, scale)
        inverse = jnp.where(fits, inverse * 2.0**-bits, inverse)
    return scale, inverse


def split_table(rows, scale):
    scaled = rows * scale
    high = scaled.astype(F8)
    low = ((scaled - high.astype(F32)) * 16.0).astype(F8)
    return jnp.concatenate([high, low], axis=1)


def build_tables(sizes, refs, table, small_table, inverses, wide=None):
    mid, top = sizes[1:]
    parts = [ref[...].astype(F32) for ref in refs]
    level, at = [], 0
    for i, size in enumerate(sizes):
        rows = jnp.concatenate([p[at : at + size] for p in parts], axis=0)
        scale, inverse = power_scale(jnp.max(jnp.abs(rows)))
        inverses[i] = inverse
        level.append(split_table(rows, scale).astype(F32))
        at += size
        if i == 0 and wide is not None:
            fixed = jnp.round(rows.T * (scale * 64.0)).astype(jnp.int32).reshape(-1, 2, 8, rows.shape[0])
            wide[...] = ((fixed[:, 0] << 16) | (fixed[:, 1] & 65535)).reshape(wide.shape)
    table[...] = level[0].astype(F8)
    pad = small_table.shape[0] - 3 * (mid + top)
    level.append(jnp.zeros((pad, level[0].shape[1]), F32))
    small_table[...] = jnp.concatenate(level[1:], axis=0).astype(F8)


def build_records(refs, sources, targets):
    blocks, _, points = refs[0].shape
    row = lax.broadcasted_iota(jnp.int32, (8, points), 0)
    empty = jnp.zeros((4, points), F32)
    for place, ref in enumerate(refs):

        @pl.loop(0, blocks // 8)
        def _(i):
            for u in range(8):
                b = i * 8 + u
                x = ref[b]
                norm = x[0:1] * x[0:1] + x[1:2] * x[1:2] + x[2:3] * x[2:3]
                x = jnp.concatenate([x, empty], axis=0)
                sources[place * blocks + b] = jnp.where(
                    row < 4, x, jnp.where(row == 4, norm, jnp.where(row == 5, 1.0, 0.0))
                )
                targets[place * blocks + b] = jnp.where(
                    row < 3, -2.0 * x, jnp.where(row == 4, 1.0, jnp.where(row == 5, norm + soften_sq, 0.0))
                )


def small_pick(column, small_table, points):
    within = (column & 255).astype(BF16)
    lanes = lax.broadcasted_iota(jnp.int32, (1, 128), 1).astype(BF16)
    halves = [jnp.where(within == i, BF16(1), BF16(0)).astype(F8) for i in (lanes, lanes + BF16(128))]
    few = jnp.dot(jnp.concatenate(halves, axis=1), small_table[...], preferred_element_type=F32)
    return (few[:, :points] + few[:, points:] * (1.0 / 16.0)).astype(BF16)


def lane_product(offset, base, count, leaf, lists_ref, rows_ref, op_ref, opt_ref, wide, small_table, picks):
    points = op_ref.shape[1]
    first = base + offset
    chunk = lists_ref[leaf:, pl.ds(pl.multiple_of(first // 128 * 128, 128), 128)]
    flat, few = None, None
    for pair in range(count // 2):
        small = []
        for j in range(2):
            v = first + 2 * pair + j
            lane = lax.rem(v, 128)
            column = jnp.take_along_axis(chunk, jnp.full(chunk.shape, lane, jnp.int32), axis=1)
            small.append(small_pick(column, small_table, points))
            for at in range(0, leaf, 128):
                row = jnp.broadcast_to(rows_ref[offset + 2 * pair + j, :, at : at + 128], (8, 128))
                tile, within = row >> 7, row & 127
                here = [tile == k for k in range(wide.shape[1] // 128)]
                for q in range(0, wide.shape[0], 8):
                    found = jnp.zeros((8, 128), jnp.int32)
                    for k, mask in enumerate(here):
                        one = jnp.take_along_axis(wide[q : q + 8, k * 128 : k * 128 + 128], within, axis=1)
                        found = jnp.where(mask, one, found)
                    both = [(found >> 16).astype(F32), ((found << 16) >> 16).astype(F32)]
                    d = j * points + 2 * q
                    picks[pair, d : d + 16, at : at + 128] = jnp.concatenate(both, axis=0).astype(BF16)
        turned = jnp.concatenate([opt_ref[offset + 2 * pair + j] for j in range(2)], axis=1)
        y = jnp.dot(turned, picks[pair], preferred_element_type=F32)
        flat = y if flat is None else flat + y
        weights = op_ref[pl.ds(first + 2 * pair, 2)].reshape(2 * points, points)
        z = jnp.dot(jnp.concatenate(small, axis=1), weights, preferred_element_type=F32)
        few = z if few is None else few + z
    return flat, few


def gather_product(first, start, count, leaf, lists_ref, op_ref, table, small_table):
    points = op_ref.shape[1]
    lanes = lax.broadcasted_iota(jnp.int32, (1, 128), 1).astype(BF16)
    ids = (lanes, lanes + BF16(128))
    one, zero = BF16(1), BF16(0)
    chunk = lists_ref[:, pl.ds(pl.multiple_of(first // 128 * 128, 128), 128)]
    result = None
    for pair in range(count // 2):
        picked = []
        for j in (2 * pair, 2 * pair + 1):
            lane = lax.rem(first + j, 128)
            column = jnp.take_along_axis(chunk, jnp.full(chunk.shape, lane, jnp.int32), axis=1)
            tile = (column >> 8).astype(BF16)
            within = (column & 255).astype(BF16)
            halves = [jnp.where(within == i, one, zero) for i in ids]
            pieces = [
                jnp.where(tile[:leaf] == BF16(k), half[:leaf], zero).astype(F8)
                for k in range(table.shape[0] // 256)
                for half in halves
            ]
            parts = jnp.dot(jnp.concatenate(pieces, axis=1), table[...], preferred_element_type=F32)
            few = jnp.dot(
                jnp.concatenate([half[leaf:].astype(F8) for half in halves], axis=1),
                small_table[...],
                preferred_element_type=F32,
            )
            both = [p[:, :points] + p[:, points:] * (1.0 / 16.0) for p in (parts, few)]
            picked.append(jnp.concatenate([b.astype(BF16) for b in both], axis=0))
        weights = op_ref[pl.ds(first - start + 2 * pair, 2)].reshape(2 * points, points)
        product = jnp.dot(jnp.concatenate(picked, axis=1), weights, preferred_element_type=F32)
        result = product if result is None else result + product
    return result


def three_parts(x):
    first = x.astype(BF16).astype(F32)
    rest = x - first
    second = rest.astype(BF16).astype(F32)
    return first, second, rest - second


def pair_term(k, pairs_ref, sources, targets):
    points = sources.shape[2]
    t, s = pairs_ref[0, k], pairs_ref[1, k]
    source = sources[s]
    s1, s2, s3 = three_parts(source)
    t1, t2, t3 = three_parts(targets[t])
    left = jnp.concatenate([s1, s1, s2, s2, s1, s3], axis=0).astype(BF16)
    right = jnp.concatenate([t1, t2, t1, t2, t3, t1], axis=0).astype(BF16)
    dist_sq = lax.dot_general(left, right, (((0,), (0,)), ((), ())), preferred_element_type=F32)
    inverse = lax.rsqrt(dist_sq)
    at_row = lax.broadcasted_iota(jnp.int32, (48, 128), 0)
    pick = jnp.where((at_row == 3) | (at_row == 19) | (at_row == 43), 1.0, 0.0).astype(BF16)
    turned = jnp.broadcast_to(source[3:4, :128], (128, 128)).T
    summed = lax.dot_general(left[:, 128:], pick, (((0,), (0,)), ((), ())), preferred_element_type=F32)
    charge = jnp.concatenate([turned, summed], axis=0)
    terms = jnp.concatenate([inverse[:, at : at + 128] * charge for at in range(0, points, 128)], axis=1)
    return t, jnp.sum(jnp.sum(terms.reshape(points // 8, 8, points), axis=0), axis=0, keepdims=True)


def translate_kernel(sizes, start, spans, *refs):
    leaf, mid, top = sizes
    lists_ref, prev_ref, own_ref, next_ref, op_ref = refs[:5]
    lanes = sum(span[0] * span[2] for span in spans)
    refs = refs[5:]
    if lanes:
        rows_ref, opt_ref, leaf_ref, mid_ref, top_ref, table, small_table, total, inverses, wide, picks, flat = refs
        flat[...] = jnp.zeros_like(flat)
        base = op_ref.shape[0] - lanes
    else:
        leaf_in, mid_in, top_in, leaf_ref, mid_ref, top_ref, table, small_table, total, inverses = refs
        wide = None
    total[...] = jnp.zeros_like(total)
    build_tables(sizes, (prev_ref, own_ref, next_ref), table, small_table, inverses, wide)
    first, turned = 0, 0
    for steps, vectors, lane_vectors in spans:

        def one(i, first=first, turned=turned, vectors=vectors, lane_vectors=lane_vectors):
            total[...] += gather_product(
                start + first + i * vectors, start, vectors, leaf, lists_ref, op_ref, table, small_table
            )
            if lane_vectors:
                more, few = lane_product(
                    turned + i * lane_vectors, base, lane_vectors, leaf,
                    lists_ref, rows_ref, op_ref, opt_ref, wide, small_table, picks,
                )
                flat[...] += more
                total[leaf:] += few

        pl.loop(0, steps)(one)
        first += steps * vectors
        turned += steps * lane_vectors
    leaf_sum, mid_sum, top_sum = total[:leaf], total[leaf : leaf + mid], total[leaf + mid : leaf + mid + top]
    if lanes:
        leaf_ref[...] = (leaf_sum + flat[...].T * (1.0 / 64.0)) * inverses[0]
        mid_ref[...] = mid_sum * inverses[1]
        top_ref[...] = top_sum * inverses[2]
    else:
        leaf_ref[...] = leaf_in[...] + leaf_sum * inverses[0]
        mid_ref[...] = mid_in[...] + mid_sum * inverses[1]
        top_ref[...] = top_in[...] + top_sum * inverses[2]


def joined_lists(lists, vectors):
    leaf, mid, top = (x.shape[0] for x in lists)
    small = -(-(mid + top) // 32) * 32
    width = -(-vectors // 128) * 128
    shifted = jnp.where(lists[2] >= 0, lists[2] + 3 * mid, -1)
    rows = jnp.concatenate([lists[0], lists[1], shifted], axis=0)
    return jnp.pad(rows, ((0, leaf + small - rows.shape[0]), (0, width - vectors)), constant_values=-1)


def translate(name, sizes, start, spans, rows, dens, operators, others):
    points = operators.shape[1]
    leaf = sizes[0]
    small = rows.shape[0] - leaf
    vmem = pl.BlockSpec(memory_space=pltpu.VMEM)
    scratch = [
        pltpu.VMEM((3 * leaf, 2 * points), F8),
        pltpu.VMEM((256, 2 * points), F8),
        pltpu.VMEM((leaf + small, points), F32),
        pltpu.SMEM((3,), F32),
    ]
    most = max(span[2] for span in spans)
    if most:
        scratch += [
            pltpu.VMEM((points // 2, 3 * leaf), jnp.int32),
            pltpu.VMEM((most // 2, 2 * points, leaf), BF16),
            pltpu.VMEM((points, leaf), F32),
        ]
    count = sum(span[0] * (span[1] + span[2]) for span in spans)
    return pl.pallas_call(
        functools.partial(translate_kernel, sizes, start, spans),
        in_specs=[vmem] * (5 + len(others)),
        out_specs=[vmem] * 3,
        out_shape=[jax.ShapeDtypeStruct((s, points), F32) for s in sizes],
        scratch_shapes=scratch,
        compiler_params=pltpu.CompilerParams(vmem_limit_bytes=40 << 20),
        cost_estimate=pl.CostEstimate(
            flops=2 * count * leaf * 2 * points * 3 * leaf, bytes_accessed=operators.size * 2, transcendentals=0
        ),
        name=name,
    )(rows, *dens, operators, *others)


def near_kernel(pairs_ref, prev_ref, own_ref, next_ref, sums_ref, sources, targets):
    sums_ref[...] = jnp.zeros_like(sums_ref)
    build_records((prev_ref, own_ref, next_ref), sources, targets)

    @pl.loop(0, pairs_ref.shape[1] // PAIR_UNROLL)
    def _(i):
        found = [pair_term(i * PAIR_UNROLL + u, pairs_ref, sources, targets) for u in range(PAIR_UNROLL)]
        for t, term in found:
            sums_ref[pl.ds(t, 1), :] += term


def near_sums(pairs, before, own, after):
    blocks, _, points = own.shape
    vmem = pl.BlockSpec(memory_space=pltpu.VMEM)
    return pl.pallas_call(
        near_kernel,
        in_specs=[pl.BlockSpec(memory_space=pltpu.SMEM), vmem, vmem, vmem],
        out_specs=vmem,
        out_shape=jax.ShapeDtypeStruct((3 * blocks, points), F32),
        scratch_shapes=[pltpu.VMEM((3 * blocks, 8, points), F32)] * 2,
        compiler_params=pltpu.CompilerParams(vmem_limit_bytes=40 << 20),
        cost_estimate=pl.CostEstimate(
            flops=pairs.shape[1] * points * points * 100, bytes_accessed=own.size * 16, transcendentals=0
        ),
        name="near_sums",
    )(pairs, before, own, after)


def body(
    leaf_density,
    mid_density,
    top_density,
    leaf_lists,
    mid_lists,
    top_lists,
    operators,
    positions,
    charges,
    pairs,
):
    blocks = positions.shape[0]
    vectors, points, _ = operators.shape
    sizes = (leaf_density.shape[0], mid_density.shape[0], top_density.shape[0])
    densities = jnp.concatenate([leaf_density, mid_density, top_density], axis=0)
    dens_before, dens_after = halo(densities)
    packed = jnp.concatenate([positions, charges[:, None, :]], axis=1)
    pack_before, pack_after = halo(packed)
    dens = (dens_before, densities, dens_after)

    rows = joined_lists((leaf_lists, mid_lists, top_lists), vectors)
    lanes = sum(span[0] * span[2] for span in SPANS)
    tail = sum(span[0] * span[1] for span in LAST_SPANS)
    at = vectors - lanes - tail
    lane_rows = leaf_lists[:, vectors - lanes :].T[:, None, :]
    turned = operators[vectors - lanes :].transpose(0, 2, 1)
    tail_operators = operators[at : at + tail]

    some = translate("translate", sizes, 0, SPANS, rows, dens, operators, (lane_rows, turned))
    some, near_in = lax.optimization_barrier((some, (pack_before, packed, pack_after)))
    offset = (lax.axis_index(AXES) - 1) * blocks
    sums = near_sums((pairs - offset).T, *near_in)
    sums, some = lax.optimization_barrier((sums, some))
    count = lax.axis_size(AXES)
    from_next = lax.ppermute(sums[:blocks], AXES, [(i + 1, i) for i in range(count - 1)])
    from_prev = lax.ppermute(sums[2 * blocks :], AXES, [(i, i + 1) for i in range(count - 1)])
    far = translate("translate_rest", sizes, at, LAST_SPANS, rows, dens, tail_operators, tuple(some))
    near_potential = sums[blocks : 2 * blocks] + from_next + from_prev
    return (*far, near_potential)


def solution(mesh):
    rows, blocks = P(AXES, None), P(AXES, None, None)
    return jax.shard_map(
        body,
        mesh=mesh,
        in_specs=(rows, rows, rows, rows, rows, rows, P(), blocks, rows, rows),
        out_specs=(rows, rows, rows, rows),
        check_vma=False,
    )
```

```python
import functools

import jax
import jax.numpy as jnp
from jax import lax
from jax.experimental import pallas as pl
from jax.experimental.pallas import tpu as pltpu
from jax.sharding import PartitionSpec as P

soften_sq = 0.0025
AXES = ("gx", "gy")
F8 = jnp.float8_e4m3fn
BF16 = jnp.bfloat16
F32 = jnp.float32
PAIR_UNROLL = 16
SPANS = ((24, 8, 4), (1, 4, 0))
LAST_SPANS = ((3, 8, 0),)


def halo(block):
    count = lax.axis_size(AXES)
    before = lax.ppermute(block, AXES, [(i, i + 1) for i in range(count - 1)])
    after = lax.ppermute(block, AXES, [(i + 1, i) for i in range(count - 1)])
    return before, after


def power_scale(largest):
    scale, inverse = jnp.float32(2.0**-119), jnp.float32(2.0**119)
    for bits in (64, 64, 32, 16, 8, 4, 2, 1):
        fits = largest * (scale * 2.0**bits) <= 448.0
        scale = jnp.where(fits, scale * 2.0**bits, scale)
        inverse = jnp.where(fits, inverse * 2.0**-bits, inverse)
    return scale, inverse


def split_table(rows, scale):
    scaled = rows * scale
    high = scaled.astype(F8)
    low = ((scaled - high.astype(F32)) * 16.0).astype(F8)
    return jnp.concatenate([high, low], axis=1)


def build_tables(sizes, refs, table, small_table, inverses, wide=None):
    mid, top = sizes[1:]
    parts = [ref[...].astype(F32) for ref in refs]
    level, at = [], 0
    for i, size in enumerate(sizes):
        rows = jnp.concatenate([p[at : at + size] for p in parts], axis=0)
        scale, inverse = power_scale(jnp.max(jnp.abs(rows)))
        inverses[i] = inverse
        level.append(split_table(rows, scale).astype(F32))
        at += size
        if i == 0 and wide is not None:
            fixed = jnp.round(rows.T * (scale * 64.0)).astype(jnp.int32).reshape(-1, 2, 8, rows.shape[0])
            wide[...] = ((fixed[:, 0] << 16) | (fixed[:, 1] & 65535)).reshape(wide.shape)
    table[...] = level[0].astype(F8)
    pad = small_table.shape[0] - 3 * (mid + top)
    level.append(jnp.zeros((pad, level[0].shape[1]), F32))
    small_table[...] = jnp.concatenate(level[1:], axis=0).astype(F8)


def build_records(refs, sources, targets, norms):
    _, blocks, points = refs[0].shape
    row = lax.broadcasted_iota(jnp.int32, (8, points), 0)
    on = [row == i for i in range(6)]
    ones = jnp.where(on[5], 1.0, 0.0)
    turned_ones = jnp.where(on[4], 1.0, 0.0)
    for place, ref in enumerate(refs):
        norms[...] = ref[0] * ref[0] + ref[1] * ref[1] + ref[2] * ref[2]

        @pl.loop(0, blocks // 8)
        def _(i):
            for u in range(8):
                b = i * 8 + u
                rows = [jnp.broadcast_to(ref[c, pl.ds(b, 1), :], (8, points)) for c in range(4)]
                norm = jnp.broadcast_to(norms[pl.ds(b, 1), :], (8, points))
                source, target = jnp.where(on[4], norm, ones), jnp.where(on[5], norm + soften_sq, turned_ones)
                for c in range(4):
                    source = jnp.where(on[c], rows[c], source)
                    if c < 3:
                        target = jnp.where(on[c], -2.0 * rows[c], target)
                sources[place * blocks + b] = source
                targets[place * blocks + b] = target


def small_pick(column, small_table, points):
    within = (column & 255).astype(BF16)
    lanes = lax.broadcasted_iota(jnp.int32, (1, 128), 1).astype(BF16)
    halves = [jnp.where(within == i, BF16(1), BF16(0)).astype(F8) for i in (lanes, lanes + BF16(128))]
    few = jnp.dot(jnp.concatenate(halves, axis=1), small_table[...], preferred_element_type=F32)
    return (few[:, :points] + few[:, points:] * (1.0 / 16.0)).astype(BF16)


def lane_product(first, count, leaf, lists_ref, rows_ref, op_ref, wide, small_table, picks):
    points = op_ref.shape[1]
    chunk = lists_ref[leaf:, pl.ds(pl.multiple_of(first // 128 * 128, 128), 128)]
    flat, few = None, None
    for pair in range(count // 2):
        small = []
        for j in range(2):
            v = first + 2 * pair + j
            lane = lax.rem(v, 128)
            column = jnp.take_along_axis(chunk, jnp.full(chunk.shape, lane, jnp.int32), axis=1)
            small.append(small_pick(column, small_table, points))
            entries = rows_ref[pl.ds(v, 1), :]
            for at in range(0, leaf, 128):
                row = jnp.broadcast_to(entries[:, at : at + 128], (8, 128))
                tile, within = row >> 7, row & 127
                here = [tile == k for k in range(wide.shape[1] // 128)]
                for q in range(0, wide.shape[0], 8):
                    found = jnp.zeros((8, 128), jnp.int32)
                    for k, mask in enumerate(here):
                        one = jnp.take_along_axis(wide[q : q + 8, k * 128 : k * 128 + 128], within, axis=1)
                        found = jnp.where(mask, one, found)
                    both = [(found >> 16).astype(F32), ((found << 16) >> 16).astype(F32)]
                    d = j * points + 2 * q
                    picks[pair, d : d + 16, at : at + 128] = jnp.concatenate(both, axis=0).astype(BF16)
        weights = op_ref[pl.ds(first + 2 * pair, 2)].reshape(2 * points, points)
        y = lax.dot_general(weights, picks[pair], (((0,), (0,)), ((), ())), preferred_element_type=F32)
        flat = y if flat is None else flat + y
        z = jnp.dot(jnp.concatenate(small, axis=1), weights, preferred_element_type=F32)
        few = z if few is None else few + z
    return flat, few


def gather_product(first, start, count, leaf, lists_ref, op_ref, table, small_table):
    points = op_ref.shape[1]
    lanes = lax.broadcasted_iota(jnp.int32, (1, 128), 1).astype(BF16)
    ids = (lanes, lanes + BF16(128))
    one, zero = BF16(1), BF16(0)
    chunk = lists_ref[:, pl.ds(pl.multiple_of(first // 128 * 128, 128), 128)]
    result = None
    for pair in range(count // 2):
        picked = []
        for j in (2 * pair, 2 * pair + 1):
            lane = lax.rem(first + j, 128)
            column = jnp.take_along_axis(chunk, jnp.full(chunk.shape, lane, jnp.int32), axis=1)
            tile = (column >> 8).astype(BF16)
            within = (column & 255).astype(BF16)
            halves = [jnp.where(within == i, one, zero) for i in ids]
            pieces = [
                jnp.where(tile[:leaf] == BF16(k), half[:leaf], zero).astype(F8)
                for k in range(table.shape[0] // 256)
                for half in halves
            ]
            parts = jnp.dot(jnp.concatenate(pieces, axis=1), table[...], preferred_element_type=F32)
            few = jnp.dot(
                jnp.concatenate([half[leaf:].astype(F8) for half in halves], axis=1),
                small_table[...],
                preferred_element_type=F32,
            )
            both = [p[:, :points] + p[:, points:] * (1.0 / 16.0) for p in (parts, few)]
            picked.append(jnp.concatenate([b.astype(BF16) for b in both], axis=0))
        weights = op_ref[pl.ds(first - start + 2 * pair, 2)].reshape(2 * points, points)
        product = jnp.dot(jnp.concatenate(picked, axis=1), weights, preferred_element_type=F32)
        result = product if result is None else result + product
    return result


def three_parts(x):
    first = x.astype(BF16).astype(F32)
    rest = x - first
    second = rest.astype(BF16).astype(F32)
    return first, second, rest - second


def pair_term(k, pairs_ref, sources, targets):
    points = sources.shape[2]
    t, s = pairs_ref[0, k], pairs_ref[1, k]
    source = sources[s]
    s1, s2, s3 = three_parts(source)
    t1, t2, t3 = three_parts(targets[t])
    left = jnp.concatenate([s1, s1, s2, s2, s1, s3], axis=0).astype(BF16)
    right = jnp.concatenate([t1, t2, t1, t2, t3, t1], axis=0).astype(BF16)
    dist_sq = lax.dot_general(left, right, (((0,), (0,)), ((), ())), preferred_element_type=F32)
    inverse = lax.rsqrt(dist_sq)
    at_row = lax.broadcasted_iota(jnp.int32, (48, 128), 0)
    pick = jnp.where((at_row == 3) | (at_row == 19) | (at_row == 43), 1.0, 0.0).astype(BF16)
    turned = jnp.broadcast_to(source[3:4, :128], (128, 128)).T
    summed = lax.dot_general(left[:, 128:], pick, (((0,), (0,)), ((), ())), preferred_element_type=F32)
    charge = jnp.concatenate([turned, summed], axis=0)
    terms = jnp.concatenate([inverse[:, at : at + 128] * charge for at in range(0, points, 128)], axis=1)
    return t, jnp.sum(jnp.sum(terms.reshape(points // 8, 8, points), axis=0), axis=0, keepdims=True)


def join_lists(sizes, lists, lists_ref):
    leaf, mid, top = sizes
    vectors = lists[0].shape[0]
    whole = vectors // 128 * 128
    lists_ref[:leaf, :whole] = lists[0][:whole].T
    if whole < vectors:
        more = jnp.zeros((128 - vectors + whole, leaf), jnp.int32)
        lists_ref[:leaf, whole : whole + 128] = jnp.concatenate([lists[0][whole:], more], axis=0).T
    lists_ref[leaf : leaf + mid, :vectors] = lists[1][...]
    entries = lists[2][...]
    lists_ref[leaf + mid : leaf + mid + top, :vectors] = jnp.where(entries >= 0, entries + 3 * mid, -1)
    end = leaf + mid + top
    lists_ref[end:, :] = jnp.full((lists_ref.shape[0] - end, lists_ref.shape[1]), -1, jnp.int32)


def translate_kernel(sizes, start, spans, *refs):
    leaf, mid, top = sizes
    lanes = sum(span[0] * span[2] for span in spans)
    prev_ref, own_ref, next_ref, op_hbm = refs[:4]
    refs = refs[4:]
    if lanes:
        rows_ref, mid_lists, top_lists, leaf_ref, mid_ref, top_ref, lists_ref = refs[:7]
        table, small_table, total, inverses, op_ref, sem, wide, picks, flat = refs[7:]
    else:
        lists_ref, leaf_in, mid_in, top_in, leaf_ref, mid_ref, top_ref = refs[:7]
        table, small_table, total, inverses, op_ref, sem = refs[7:]
        wide = None
    fetch = pltpu.make_async_copy(op_hbm.at[pl.ds(start, op_ref.shape[0])], op_ref, sem)
    fetch.start()
    total[...] = jnp.zeros_like(total)
    if lanes:
        flat[...] = jnp.zeros_like(flat)
        join_lists(sizes, (rows_ref, mid_lists, top_lists), lists_ref)
        base = op_ref.shape[0] - lanes
    build_tables(sizes, (prev_ref, own_ref, next_ref), table, small_table, inverses, wide)
    fetch.wait()
    first, turned = 0, 0
    for steps, vectors, lane_vectors in spans:

        def one(i, first=first, turned=turned, vectors=vectors, lane_vectors=lane_vectors):
            total[...] += gather_product(
                start + first + i * vectors, start, vectors, leaf, lists_ref, op_ref, table, small_table
            )
            if lane_vectors:
                more, few = lane_product(
                    base + turned + i * lane_vectors, lane_vectors, leaf,
                    lists_ref, rows_ref, op_ref, wide, small_table, picks,
                )
                flat[...] += more
                total[leaf:] += few

        pl.loop(0, steps)(one)
        first += steps * vectors
        turned += steps * lane_vectors
    leaf_sum, mid_sum, top_sum = total[:leaf], total[leaf : leaf + mid], total[leaf + mid : leaf + mid + top]
    if lanes:
        leaf_ref[...] = (leaf_sum + flat[...].T * (1.0 / 64.0)) * inverses[0]
        mid_ref[...] = mid_sum * inverses[1]
        top_ref[...] = top_sum * inverses[2]
    else:
        leaf_ref[...] = leaf_in[...] + leaf_sum * inverses[0]
        mid_ref[...] = mid_in[...] + mid_sum * inverses[1]
        top_ref[...] = top_in[...] + top_sum * inverses[2]


def translate(name, sizes, start, spans, dens, operators, others):
    vectors, points, _ = operators.shape
    leaf, mid, top = sizes
    rows = (leaf + -(-(mid + top) // 32) * 32, -(-vectors // 128) * 128)
    vmem = pl.BlockSpec(memory_space=pltpu.VMEM)
    most = max(span[2] for span in spans)
    count = sum(span[0] * (span[1] + span[2]) for span in spans)
    scratch = [
        pltpu.VMEM((3 * leaf, 2 * points), F8),
        pltpu.VMEM((256, 2 * points), F8),
        pltpu.VMEM((rows[0], points), F32),
        pltpu.SMEM((3,), F32),
        pltpu.VMEM((vectors if most else count, points, points), BF16),
        pltpu.SemaphoreType.DMA,
    ]
    out_shape = [jax.ShapeDtypeStruct((s, points), F32) for s in sizes]
    if most:
        out_shape.append(jax.ShapeDtypeStruct(rows, jnp.int32))
        scratch += [
            pltpu.VMEM((points // 2, 3 * leaf), jnp.int32),
            pltpu.VMEM((most // 2, 2 * points, leaf), BF16),
            pltpu.VMEM((points, leaf), F32),
        ]
    return pl.pallas_call(
        functools.partial(translate_kernel, sizes, start, spans),
        in_specs=[vmem] * 3 + [pl.BlockSpec(memory_space=pl.ANY)] + [vmem] * len(others),
        out_specs=[vmem] * len(out_shape),
        out_shape=out_shape,
        scratch_shapes=scratch,
        compiler_params=pltpu.CompilerParams(vmem_limit_bytes=40 << 20),
        cost_estimate=pl.CostEstimate(
            flops=2 * count * leaf * 2 * points * 3 * leaf, bytes_accessed=operators.size * 2, transcendentals=0
        ),
        name=name,
    )(*dens, operators, *others)


def near_kernel(pairs_ref, prev_ref, own_ref, next_ref, sums_ref, sources, targets, norms):
    sums_ref[...] = jnp.zeros_like(sums_ref)
    build_records((prev_ref, own_ref, next_ref), sources, targets, norms)

    @pl.loop(0, pairs_ref.shape[1] // PAIR_UNROLL)
    def _(i):
        found = [pair_term(i * PAIR_UNROLL + u, pairs_ref, sources, targets) for u in range(PAIR_UNROLL)]
        for t, term in found:
            sums_ref[pl.ds(t, 1), :] += term


def near_sums(pairs, before, own, after):
    _, blocks, points = own.shape
    vmem = pl.BlockSpec(memory_space=pltpu.VMEM)
    return pl.pallas_call(
        near_kernel,
        in_specs=[pl.BlockSpec(memory_space=pltpu.SMEM), vmem, vmem, vmem],
        out_specs=vmem,
        out_shape=jax.ShapeDtypeStruct((3 * blocks, points), F32),
        scratch_shapes=[pltpu.VMEM((3 * blocks, 8, points), F32)] * 2 + [pltpu.VMEM((blocks, points), F32)],
        compiler_params=pltpu.CompilerParams(vmem_limit_bytes=40 << 20),
        cost_estimate=pl.CostEstimate(
            flops=pairs.shape[1] * points * points * 100, bytes_accessed=own.size * 16, transcendentals=0
        ),
        name="near_sums",
    )(pairs, before, own, after)


def body(
    leaf_density,
    mid_density,
    top_density,
    leaf_lists,
    mid_lists,
    top_lists,
    operators,
    positions,
    charges,
    pairs,
):
    blocks = positions.shape[0]
    sizes = (leaf_density.shape[0], mid_density.shape[0], top_density.shape[0])
    densities = jnp.concatenate([leaf_density, mid_density, top_density], axis=0)
    dens_before, dens_after = halo(densities)
    packed = jnp.concatenate([positions.transpose(1, 0, 2), charges[None]], axis=0)
    pack_before, pack_after = halo(packed)
    dens = (dens_before, densities, dens_after)

    first = sum(span[0] * span[1] for span in SPANS)
    lists = (leaf_lists.T, mid_lists, top_lists)
    *some, rows = translate("translate", sizes, 0, SPANS, dens, operators, lists)
    some, near_in = lax.optimization_barrier((some, (pack_before, packed, pack_after)))
    offset = (lax.axis_index(AXES) - 1) * blocks
    sums = near_sums((pairs - offset).T, *near_in)
    sums, some = lax.optimization_barrier((sums, some))
    count = lax.axis_size(AXES)
    from_next = lax.ppermute(sums[:blocks], AXES, [(i + 1, i) for i in range(count - 1)])
    from_prev = lax.ppermute(sums[2 * blocks :], AXES, [(i, i + 1) for i in range(count - 1)])
    far = translate("translate_rest", sizes, first, LAST_SPANS, dens, operators, (rows, *some))
    near_potential = sums[blocks : 2 * blocks] + from_next + from_prev
    return (*far, near_potential)


def solution(mesh):
    rows, blocks = P(AXES, None), P(AXES, None, None)
    return jax.shard_map(
        body,
        mesh=mesh,
        in_specs=(rows, rows, rows, rows, rows, rows, P(), blocks, rows, rows),
        out_specs=(rows, rows, rows, rows),
        check_vma=False,
    )
```

```python
import functools

import jax
import jax.numpy as jnp
from jax import lax
from jax.experimental import pallas as pl
from jax.experimental.pallas import tpu as pltpu
from jax.sharding import PartitionSpec as P

soften_sq = 0.0025
AXES = ("gx", "gy")
F8 = jnp.float8_e4m3fn
BF16 = jnp.bfloat16
F32 = jnp.float32
PAIR_UNROLL = 32
SPANS = ((24, 8, 4), (1, 4, 0))
LAST_SPANS = ((3, 8, 0),)


def halo(block):
    count = lax.axis_size(AXES)
    before = lax.ppermute(block, AXES, [(i, i + 1) for i in range(count - 1)])
    after = lax.ppermute(block, AXES, [(i + 1, i) for i in range(count - 1)])
    return before, after


def power_scale(largest):
    scale, inverse = jnp.float32(2.0**-119), jnp.float32(2.0**119)
    for bits in (64, 64, 32, 16, 8, 4, 2, 1):
        fits = largest * (scale * 2.0**bits) <= 448.0
        scale = jnp.where(fits, scale * 2.0**bits, scale)
        inverse = jnp.where(fits, inverse * 2.0**-bits, inverse)
    return scale, inverse


def split_table(rows, scale):
    scaled = rows * scale
    high = scaled.astype(F8)
    low = ((scaled - high.astype(F32)) * 16.0).astype(F8)
    return jnp.concatenate([high, low], axis=1)


def build_tables(sizes, refs, table, small_table, inverses, wide=None):
    mid, top = sizes[1:]
    parts = [ref[...].astype(F32) for ref in refs]
    level, at = [], 0
    for i, size in enumerate(sizes):
        rows = jnp.concatenate([p[at : at + size] for p in parts], axis=0)
        scale, inverse = power_scale(jnp.max(jnp.abs(rows)))
        inverses[i] = inverse
        level.append(split_table(rows, scale).astype(F32))
        at += size
        if i == 0 and wide is not None:
            fixed = jnp.round(rows.T * (scale * 64.0)).astype(jnp.int32).reshape(-1, 2, 8, rows.shape[0])
            wide[...] = ((fixed[:, 0] << 16) | (fixed[:, 1] & 65535)).reshape(wide.shape)
    table[...] = level[0].astype(F8)
    pad = small_table.shape[0] - 3 * (mid + top)
    level.append(jnp.zeros((pad, level[0].shape[1]), F32))
    small_table[...] = jnp.concatenate(level[1:], axis=0).astype(F8)


def build_records(refs, sources, targets, norms):
    _, blocks, points = refs[0].shape
    row = lax.broadcasted_iota(jnp.int32, (8, points), 0)
    on = [row == i for i in range(6)]
    ones = jnp.where(on[5], 1.0, 0.0)
    turned_ones = jnp.where(on[4], 1.0, 0.0)
    for place, ref in enumerate(refs):
        norms[...] = ref[0] * ref[0] + ref[1] * ref[1] + ref[2] * ref[2]

        @pl.loop(0, blocks // 8)
        def _(i):
            for u in range(8):
                b = i * 8 + u
                rows = [jnp.broadcast_to(ref[c, pl.ds(b, 1), :], (8, points)) for c in range(4)]
                norm = jnp.broadcast_to(norms[pl.ds(b, 1), :], (8, points))
                source, target = jnp.where(on[4], norm, ones), jnp.where(on[5], norm + soften_sq, turned_ones)
                for c in range(4):
                    source = jnp.where(on[c], rows[c], source)
                    if c < 3:
                        target = jnp.where(on[c], -2.0 * rows[c], target)
                sources[place * blocks + b] = source
                targets[place * blocks + b] = target


def small_pick(column, small_table, points):
    within = (column & 255).astype(BF16)
    lanes = lax.broadcasted_iota(jnp.int32, (1, 128), 1).astype(BF16)
    halves = [jnp.where(within == i, BF16(1), BF16(0)).astype(F8) for i in (lanes, lanes + BF16(128))]
    few = jnp.dot(jnp.concatenate(halves, axis=1), small_table[...], preferred_element_type=F32)
    return (few[:, :points] + few[:, points:] * (1.0 / 16.0)).astype(BF16)


def lane_product(first, count, leaf, lists_ref, rows_ref, op_ref, wide, small_table, picks):
    points = op_ref.shape[1]
    flat, few = None, None
    for pair in range(count // 2):
        small = []
        chunk = lists_ref[leaf:, pl.ds(pl.multiple_of((first + 2 * pair) // 128 * 128, 128), 128)]
        for j in range(2):
            v = first + 2 * pair + j
            lane = lax.rem(v, 128)
            column = jnp.take_along_axis(chunk, jnp.full(chunk.shape, lane, jnp.int32), axis=1)
            small.append(small_pick(column, small_table, points))
            entries = rows_ref[pl.ds(v, 1), :]
            for at in range(0, leaf, 128):
                row = jnp.broadcast_to(entries[:, at : at + 128], (8, 128))
                tile, within = row >> 7, row & 127
                here = [tile == k for k in range(wide.shape[1] // 128)]
                for q in range(0, wide.shape[0], 8):
                    found = jnp.zeros((8, 128), jnp.int32)
                    for k, mask in enumerate(here):
                        one = jnp.take_along_axis(wide[q : q + 8, k * 128 : k * 128 + 128], within, axis=1)
                        found = jnp.where(mask, one, found)
                    both = [(found >> 16).astype(F32), ((found << 16) >> 16).astype(F32)]
                    d = j * points + 2 * q
                    picks[pair, d : d + 16, at : at + 128] = jnp.concatenate(both, axis=0).astype(BF16)
        weights = op_ref[pl.ds(first + 2 * pair, 2)].reshape(2 * points, points)
        y = lax.dot_general(weights, picks[pair], (((0,), (0,)), ((), ())), preferred_element_type=F32)
        flat = y if flat is None else flat + y
        z = jnp.dot(jnp.concatenate(small, axis=1), weights, preferred_element_type=F32)
        few = z if few is None else few + z
    return flat, few


def gather_product(first, start, count, leaf, lists_ref, op_ref, table, small_table):
    points = op_ref.shape[1]
    lanes = lax.broadcasted_iota(jnp.int32, (1, 128), 1).astype(BF16)
    ids = (lanes, lanes + BF16(128))
    one, zero = BF16(1), BF16(0)
    result = None
    for pair in range(count // 2):
        picked = []
        chunk = lists_ref[:, pl.ds(pl.multiple_of((first + 2 * pair) // 128 * 128, 128), 128)]
        for j in (2 * pair, 2 * pair + 1):
            lane = lax.rem(first + j, 128)
            column = jnp.take_along_axis(chunk, jnp.full(chunk.shape, lane, jnp.int32), axis=1)
            tile = (column >> 8).astype(BF16)
            within = (column & 255).astype(BF16)
            halves = [jnp.where(within == i, one, zero) for i in ids]
            pieces = [
                jnp.where(tile[:leaf] == BF16(k), half[:leaf], zero).astype(F8)
                for k in range(table.shape[0] // 256)
                for half in halves
            ]
            parts = jnp.dot(jnp.concatenate(pieces, axis=1), table[...], preferred_element_type=F32)
            few = jnp.dot(
                jnp.concatenate([half[leaf:].astype(F8) for half in halves], axis=1),
                small_table[...],
                preferred_element_type=F32,
            )
            both = [p[:, :points] + p[:, points:] * (1.0 / 16.0) for p in (parts, few)]
            picked.append(jnp.concatenate([b.astype(BF16) for b in both], axis=0))
        weights = op_ref[pl.ds(first - start + 2 * pair, 2)].reshape(2 * points, points)
        product = jnp.dot(jnp.concatenate(picked, axis=1), weights, preferred_element_type=F32)
        result = product if result is None else result + product
    return result


def three_parts(x):
    first = x.astype(BF16).astype(F32)
    rest = x - first
    second = rest.astype(BF16).astype(F32)
    return first, second, rest - second


def pair_term(k, pairs_ref, sources, targets):
    points = sources.shape[2]
    t, s = pairs_ref[0, k], pairs_ref[1, k]
    source = sources[s]
    s1, s2, s3 = three_parts(source)
    t1, t2, t3 = three_parts(targets[t])
    left = jnp.concatenate([s1, s1, s2, s2, s1, s3], axis=0).astype(BF16)
    right = jnp.concatenate([t1, t2, t1, t2, t3, t1], axis=0).astype(BF16)
    dist_sq = lax.dot_general(left, right, (((0,), (0,)), ((), ())), preferred_element_type=F32)
    inverse = lax.rsqrt(dist_sq)
    at_row = lax.broadcasted_iota(jnp.int32, (48, 128), 0)
    pick = jnp.where((at_row == 3) | (at_row == 19) | (at_row == 43), 1.0, 0.0).astype(BF16)
    turned = jnp.broadcast_to(source[3:4, :128], (128, 128)).T
    summed = lax.dot_general(left[:, 128:], pick, (((0,), (0,)), ((), ())), preferred_element_type=F32)
    charge = jnp.concatenate([turned, summed], axis=0)
    terms = jnp.concatenate([inverse[:, at : at + 128] * charge for at in range(0, points, 128)], axis=1)
    return t, jnp.sum(jnp.sum(terms.reshape(points // 8, 8, points), axis=0), axis=0, keepdims=True)


def join_lists(sizes, lists, lists_ref):
    leaf, mid, top = sizes
    vectors = lists[0].shape[0]
    whole = vectors // 128 * 128
    lists_ref[:leaf, :whole] = lists[0][:whole].T
    if whole < vectors:
        more = jnp.zeros((128 - vectors + whole, leaf), jnp.int32)
        lists_ref[:leaf, whole : whole + 128] = jnp.concatenate([lists[0][whole:], more], axis=0).T
    lists_ref[leaf : leaf + mid, :vectors] = lists[1][...]
    entries = lists[2][...]
    lists_ref[leaf + mid : leaf + mid + top, :vectors] = jnp.where(entries >= 0, entries + 3 * mid, -1)
    end = leaf + mid + top
    lists_ref[end:, :] = jnp.full((lists_ref.shape[0] - end, lists_ref.shape[1]), -1, jnp.int32)


def translate_kernel(sizes, start, spans, *refs):
    leaf, mid, top = sizes
    lanes = sum(span[0] * span[2] for span in spans)
    prev_ref, own_ref, next_ref, op_hbm = refs[:4]
    refs = refs[4:]
    if lanes:
        rows_ref, mid_lists, top_lists, leaf_ref, mid_ref, top_ref, lists_ref = refs[:7]
        table, small_table, total, inverses, op_ref, sem, wide, picks, flat = refs[7:]
    else:
        lists_ref, leaf_in, mid_in, top_in, leaf_ref, mid_ref, top_ref = refs[:7]
        table, small_table, total, inverses, op_ref, sem = refs[7:]
        wide = None
    fetch = pltpu.make_async_copy(op_hbm.at[pl.ds(start, op_ref.shape[0])], op_ref, sem)
    fetch.start()
    total[...] = jnp.zeros_like(total)
    if lanes:
        flat[...] = jnp.zeros_like(flat)
        join_lists(sizes, (rows_ref, mid_lists, top_lists), lists_ref)
        base = op_ref.shape[0] - lanes
    build_tables(sizes, (prev_ref, own_ref, next_ref), table, small_table, inverses, wide)
    fetch.wait()
    first, turned = 0, 0
    for steps, vectors, lane_vectors in spans:

        def one(i, first=first, turned=turned, vectors=vectors, lane_vectors=lane_vectors):
            total[...] += gather_product(
                start + first + i * vectors, start, vectors, leaf, lists_ref, op_ref, table, small_table
            )
            if lane_vectors:
                more, few = lane_product(
                    base + turned + i * lane_vectors, lane_vectors, leaf,
                    lists_ref, rows_ref, op_ref, wide, small_table, picks,
                )
                flat[...] += more
                total[leaf:] += few

        pl.loop(0, steps)(one)
        first += steps * vectors
        turned += steps * lane_vectors
    leaf_sum, mid_sum, top_sum = total[:leaf], total[leaf : leaf + mid], total[leaf + mid : leaf + mid + top]
    if lanes:
        leaf_ref[...] = (leaf_sum + flat[...].T * (1.0 / 64.0)) * inverses[0]
        mid_ref[...] = mid_sum * inverses[1]
        top_ref[...] = top_sum * inverses[2]
    else:
        leaf_ref[...] = leaf_in[...] + leaf_sum * inverses[0]
        mid_ref[...] = mid_in[...] + mid_sum * inverses[1]
        top_ref[...] = top_in[...] + top_sum * inverses[2]


def translate(name, sizes, start, spans, dens, operators, others):
    vectors, points, _ = operators.shape
    leaf, mid, top = sizes
    rows = (leaf + -(-(mid + top) // 32) * 32, -(-vectors // 128) * 128)
    vmem = pl.BlockSpec(memory_space=pltpu.VMEM)
    most = max(span[2] for span in spans)
    count = sum(span[0] * (span[1] + span[2]) for span in spans)
    scratch = [
        pltpu.VMEM((3 * leaf, 2 * points), F8),
        pltpu.VMEM((256, 2 * points), F8),
        pltpu.VMEM((rows[0], points), F32),
        pltpu.SMEM((3,), F32),
        pltpu.VMEM((vectors if most else count, points, points), BF16),
        pltpu.SemaphoreType.DMA,
    ]
    out_shape = [jax.ShapeDtypeStruct((s, points), F32) for s in sizes]
    if most:
        out_shape.append(jax.ShapeDtypeStruct(rows, jnp.int32))
        scratch += [
            pltpu.VMEM((points // 2, 3 * leaf), jnp.int32),
            pltpu.VMEM((most // 2, 2 * points, leaf), BF16),
            pltpu.VMEM((points, leaf), F32),
        ]
    return pl.pallas_call(
        functools.partial(translate_kernel, sizes, start, spans),
        in_specs=[vmem] * 3 + [pl.BlockSpec(memory_space=pltpu.HBM)] + [vmem] * len(others),
        out_specs=[vmem] * len(out_shape),
        out_shape=out_shape,
        scratch_shapes=scratch,
        compiler_params=pltpu.CompilerParams(vmem_limit_bytes=56 << 20),
        cost_estimate=pl.CostEstimate(
            flops=2 * count * leaf * 2 * points * 3 * leaf, bytes_accessed=operators.size * 2, transcendentals=0
        ),
        name=name,
    )(*dens, operators, *others)


def near_kernel(pairs_ref, prev_ref, own_ref, next_ref, sums_ref, sources, targets, norms):
    sums_ref[...] = jnp.zeros_like(sums_ref)
    build_records((prev_ref, own_ref, next_ref), sources, targets, norms)

    @pl.loop(0, pairs_ref.shape[1] // PAIR_UNROLL)
    def _(i):
        found = [pair_term(i * PAIR_UNROLL + u, pairs_ref, sources, targets) for u in range(PAIR_UNROLL)]
        for t, term in found:
            sums_ref[pl.ds(t, 1), :] += term


def near_sums(pairs, before, own, after):
    _, blocks, points = own.shape
    vmem = pl.BlockSpec(memory_space=pltpu.VMEM)
    return pl.pallas_call(
        near_kernel,
        in_specs=[pl.BlockSpec(memory_space=pltpu.SMEM), vmem, vmem, vmem],
        out_specs=vmem,
        out_shape=jax.ShapeDtypeStruct((3 * blocks, points), F32),
        scratch_shapes=[pltpu.VMEM((3 * blocks, 8, points), F32)] * 2 + [pltpu.VMEM((blocks, points), F32)],
        compiler_params=pltpu.CompilerParams(vmem_limit_bytes=40 << 20),
        cost_estimate=pl.CostEstimate(
            flops=pairs.shape[1] * points * points * 100, bytes_accessed=own.size * 16, transcendentals=0
        ),
        name="near_sums",
    )(pairs, before, own, after)


def body(
    leaf_density,
    mid_density,
    top_density,
    leaf_lists,
    mid_lists,
    top_lists,
    operators,
    positions,
    charges,
    pairs,
):
    blocks = positions.shape[0]
    sizes = (leaf_density.shape[0], mid_density.shape[0], top_density.shape[0])
    densities = jnp.concatenate([leaf_density, mid_density, top_density], axis=0)
    dens_before, dens_after = halo(densities)
    packed = jnp.concatenate([positions.transpose(1, 0, 2), charges[None]], axis=0)
    pack_before, pack_after = halo(packed)
    dens = (dens_before, densities, dens_after)

    first = sum(span[0] * span[1] for span in SPANS)
    lists = (leaf_lists.T, mid_lists, top_lists)
    *some, rows = translate("translate", sizes, 0, SPANS, dens, operators, lists)
    some, near_in = lax.optimization_barrier((some, (pack_before, packed, pack_after)))
    offset = (lax.axis_index(AXES) - 1) * blocks
    sums = near_sums((pairs - offset).T, *near_in)
    sums, some = lax.optimization_barrier((sums, some))
    count = lax.axis_size(AXES)
    from_next = lax.ppermute(sums[:blocks], AXES, [(i + 1, i) for i in range(count - 1)])
    from_prev = lax.ppermute(sums[2 * blocks :], AXES, [(i, i + 1) for i in range(count - 1)])
    far = translate("translate_rest", sizes, first, LAST_SPANS, dens, operators, (rows, *some))
    near_potential = sums[blocks : 2 * blocks] + from_next + from_prev
    return (*far, near_potential)


def solution(mesh):
    rows, blocks = P(AXES, None), P(AXES, None, None)
    return jax.shard_map(
        body,
        mesh=mesh,
        in_specs=(rows, rows, rows, rows, rows, rows, P(), blocks, rows, rows),
        out_specs=(rows, rows, rows, rows),
        check_vma=False,
    )
```
